32 devices in a mesh: dp: 4 (over y, core), ctx: 2 (over x), seq: 4 (over z).
Axes of the slice: x: 2, y: 2, z: 4, core: 2. Of those that a mesh axis runs over, the one named last changes fastest.
Arguments:
- inputs: bfloat16 [5120, 2304], P(('dp', 'ctx', 'seq')), may hold values from -6 to 6
- positions: int32 [5120], P(('dp', 'ctx')), may hold values from 0 to 4959, as said below
- w_query: bfloat16 [2304, 2048], P(('dp', 'ctx')), may hold values from -0.25 to 0.25
- key_weight: bfloat16 [2304, 1024], P(('dp', 'ctx')), may hold values from -0.1875 to 0.1875
- value_weight: bfloat16 [2304, 1024], P(('dp', 'ctx')), may hold values from -0.125 to 0.125
- w_out: bfloat16 [2304, 2048], P(('dp', 'ctx')), may hold values from -0.125 to 0.125
- w_gate: bfloat16 [9216, 2304], P(('dp', 'ctx')), may hold values from -0.125 to 0.125
- w_up: bfloat16 [9216, 2304], P(('dp', 'ctx')), may hold values from -0.125 to 0.125
- w_down: bfloat16 [9216, 2304], P(('dp', 'ctx')), may hold values from -0.0625 to 0.0625
- gain_attn_in: float32 [2304], replicated, may hold values from -0.75 to 0.75
- gain_attn_out: float32 [2304], replicated, may hold values from -0.75 to 0.75
- gain_ffn_in: float32 [2304], replicated, may hold values from -0.75 to 0.75
- gain_ffn_out: float32 [2304], replicated, may hold values from -0.75 to 0.75
- cotangent: bfloat16 [5120, 2304], P(('dp', 'ctx', 'seq')), may hold values from -6 to 6
Outputs:
- output: float32 [5120, 2304], P(('dp', 'ctx', 'seq'))
- grad_inputs: float32 [5120, 2304], P(('dp', 'ctx', 'seq'))
- grad_w_query: float32 [2304, 2048], P(('dp', 'ctx'))
- grad_w_key: float32 [2304, 1024], P(('dp', 'ctx'))
- grad_w_value: float32 [2304, 1024], P(('dp', 'ctx'))
- grad_w_out: float32 [2304, 2048], P(('dp', 'ctx'))
- grad_w_gate: float32 [9216, 2304], P(('dp', 'ctx'))
- grad_w_up: float32 [9216, 2304], P(('dp', 'ctx'))
- grad_w_down: float32 [9216, 2304], P(('dp', 'ctx'))
- grad_gain_attn_in: float32 [2304], replicated
- grad_gain_attn_out: float32 [2304], replicated
- grad_gain_ffn_in: float32 [2304], replicated
- grad_gain_ffn_out: float32 [2304], replicated
The draws below stay inside these ranges and needn't reach their ends.
Inputs may be any that keep to these rules, and one draw needn't show every extreme that they name: `positions`: positions count from 0 within each packed document. One document has exactly 4960 tokens and reaches from the first device to the last; the documents before it lie within the first 160 tokens and those after it within the last 160 tokens, in one or more short documents of varying lengths.
All inputs are finite; a program needn't handle non-finite values.
Results may differ from the reference program's by a relative error of at most 0.025.
Values may be sent and summed in bfloat16 or wider, within the bound.
A program may use at most 704 MiB of HBM per device.

```python
import math
import jax
import jax.numpy as jnp
from jax import lax

MODEL_DIMENSION = 2304
FF = 9216
QUERY_HEADS = 8
KEY_VALUE_HEADS = 4
HEAD_SIZE = 256
WINDOW = 4096
TOK_DEV = 160
BLOCK_TOKENS = 640
SEQUENCE_LENGTH = 5120
BACK_BLOCKS = 7


def draw_positions(key, part):
    key = jax.random.fold_in(key, 11)
    first_end = jax.random.randint(jax.random.fold_in(key, 1), (), 1, TOK_DEV)
    last_start = first_end + (SEQUENCE_LENGTH - TOK_DEV)
    token_index = jnp.arange(SEQUENCE_LENGTH, dtype=jnp.int32)
    flags = jax.random.randint(jax.random.fold_in(key, 2), (SEQUENCE_LENGTH,), 0, 3) == 0
    short_zone = (token_index < first_end) | (token_index > last_start)
    starts = (token_index == 0) | (token_index == first_end) | (token_index == last_start) | flags & short_zone
    doc_start = lax.cummax(jnp.where(starts, token_index, 0).astype(jnp.int32), axis=0)
    return (token_index - doc_start).astype(jnp.int32)


def level_of(key, extent, cuts, least, high):
    gain, own = 1.0, jax.random.fold_in(key, 6)
    for axis_at, shards_of in cuts:
        draws = jnp.exp(jax.random.uniform(jax.random.fold_in(own, axis_at), (shards_of,), jnp.float32, least / len(cuts), high / len(cuts)))
        gain = gain * jnp.repeat(draws, extent[axis_at] // shards_of).reshape([-1 if axis == axis_at else 1 for axis in range(len(extent))])
    return gain


def centred(key, shape, spread, reach, split=(), kind=jnp.bfloat16):
    drawn = spread * jax.random.normal(key, shape, jnp.float32)
    if split:
        drawn = drawn * level_of(key, shape, split, -0.22, 0.18)
    return jnp.clip(drawn, -reach, reach).astype(kind)


def setup_inputs(seed: int = 0) -> dict:
    key_list = jax.random.split(jax.random.key(seed), 15)
    inputs = centred(key_list[0], (SEQUENCE_LENGTH, MODEL_DIMENSION), 1.0, 6.0, ((0, 32),))
    positions = draw_positions(jax.random.fold_in(key_list[14], 71), 0)
    w_query = centred(key_list[2], (MODEL_DIMENSION, QUERY_HEADS * HEAD_SIZE), (MODEL_DIMENSION // 4) ** -0.5, 0.25, ((0, 8),))
    key_weight = centred(key_list[3], (MODEL_DIMENSION, KEY_VALUE_HEADS * HEAD_SIZE), (MODEL_DIMENSION // 2) ** -0.5, 0.1875, ((0, 8),))
    value_weight = centred(key_list[4], (MODEL_DIMENSION, KEY_VALUE_HEADS * HEAD_SIZE), MODEL_DIMENSION ** -0.5, 0.125, ((0, 8),))
    w_out = centred(key_list[5], (MODEL_DIMENSION, QUERY_HEADS * HEAD_SIZE), (QUERY_HEADS * HEAD_SIZE) ** -0.5, 0.125, ((0, 8),))
    w_gate = centred(key_list[6], (FF, MODEL_DIMENSION), MODEL_DIMENSION ** -0.5, 0.125, ((0, 8),))
    w_up = centred(key_list[7], (FF, MODEL_DIMENSION), MODEL_DIMENSION ** -0.5, 0.125, ((0, 8),))
    w_down = centred(key_list[8], (FF, MODEL_DIMENSION), FF ** -0.5, 0.0625, ((0, 8),))
    gain_attn_in = centred(key_list[9], (MODEL_DIMENSION,), 0.15, 0.75, (), jnp.float32)
    gain_attn_out = centred(key_list[10], (MODEL_DIMENSION,), 0.15, 0.75, (), jnp.float32)
    gain_ffn_in = centred(key_list[11], (MODEL_DIMENSION,), 0.15, 0.75, (), jnp.float32)
    gain_ffn_out = centred(key_list[12], (MODEL_DIMENSION,), 0.15, 0.75, (), jnp.float32)
    cotangent = centred(key_list[13], (SEQUENCE_LENGTH, MODEL_DIMENSION), 1.0, 6.0, ((0, 32),))
    return dict(inputs=inputs, positions=positions, w_query=w_query, key_weight=key_weight, value_weight=value_weight, w_out=w_out, w_gate=w_gate, w_up=w_up, w_down=w_down, gain_attn_in=gain_attn_in, gain_attn_out=gain_attn_out, gain_ffn_in=gain_ffn_in, gain_ffn_out=gain_ffn_out, cotangent=cotangent)


NORM_EPS = 1e-06
SOFT_CAP = 50.0
PRECISION_LEVEL = lax.Precision.HIGHEST

@jax.custom_vjp
def reduced_copy(v):
    return lax.optimization_barrier(v.astype(jnp.bfloat16)).astype(jnp.float32)

@jax.custom_vjp
def reduced_backward(v):
    return v

def low_keep(v):
    return (reduced_copy(v), None)

def low_pass(kept, grad):
    return (grad,)

def back_keep(v):
    return (v, None)

def back_low(kept, grad):
    return (reduced_copy(grad),)
reduced_copy.defvjp(low_keep, low_pass)
reduced_backward.defvjp(back_keep, back_low)

def normed(values, gain_vec):
    return values * lax.rsqrt(lax.optimization_barrier(jnp.mean(values * values, axis=-1, keepdims=True)) + NORM_EPS) * (1.0 + gain_vec)

def gelu_tanh(values):
    return jax.nn.gelu(values, approximate=True)

def angles(pos_rows, head_dim):
    frequency = jnp.exp(jnp.arange(head_dim // 2, dtype=jnp.float32) * (-2.0 * math.log(10000.0) / head_dim))
    turned = pos_rows.astype(jnp.float32)[:, None] * frequency[None, :]
    return (jnp.cos(turned)[:, None, :], jnp.sin(turned)[:, None, :])

def rotate(values, cos_part, sin_part):
    half_dim = values.shape[-1] // 2
    first_half = values[..., :half_dim]
    second_half = values[..., half_dim:]
    return jnp.concatenate([first_half * cos_part - second_half * sin_part, second_half * cos_part + first_half * sin_part], axis=-1)

def attend(query_values, key, value_vectors, positions):
    count_of_blocks = SEQUENCE_LENGTH // BLOCK_TOKENS
    grouping_factor = QUERY_HEADS // KEY_VALUE_HEADS
    padding_rows = BACK_BLOCKS * BLOCK_TOKENS
    span_rows = padding_rows + BLOCK_TOKENS
    padded_keys = jnp.concatenate([jnp.zeros((padding_rows, KEY_VALUE_HEADS, HEAD_SIZE), jnp.float32), key], axis=0)
    padded_values = jnp.concatenate([jnp.zeros((padding_rows, KEY_VALUE_HEADS, HEAD_SIZE), jnp.float32), value_vectors], axis=0)
    blocked_queries = query_values.reshape(count_of_blocks, BLOCK_TOKENS, KEY_VALUE_HEADS, grouping_factor, HEAD_SIZE)
    position_blocks = positions.reshape(count_of_blocks, BLOCK_TOKENS)
    score_scale = HEAD_SIZE ** (-0.5)

    def one_block(packed):
        block_index, query_block, position_block = packed
        row_start = (block_index * BLOCK_TOKENS).astype(jnp.int32)
        key_span = lax.dynamic_slice_in_dim(padded_keys, row_start, span_rows, 0)
        value_span = lax.dynamic_slice_in_dim(padded_values, row_start, span_rows, 0)
        raw_scores = reduced_backward(jnp.einsum('rkgd,ckd->kgrc', query_block, key_span, precision=PRECISION_LEVEL))
        capped = SOFT_CAP * jnp.tanh(raw_scores * score_scale / SOFT_CAP)
        row_ids = row_start + jnp.arange(BLOCK_TOKENS, dtype=jnp.int32)
        col_ids = row_start - padding_rows + jnp.arange(span_rows, dtype=jnp.int32)
        lower_ids = row_ids - jnp.minimum(position_block, WINDOW - 1)
        allowed = (col_ids[None, :] <= row_ids[:, None]) & (col_ids[None, :] >= lower_ids[:, None])
        masked = jnp.where(allowed, capped, -1e+30)
        row_top = lax.optimization_barrier(jnp.max(masked, axis=-1, keepdims=True))
        log_total = row_top + jnp.log(lax.optimization_barrier(jnp.sum(jnp.exp(masked - row_top), axis=-1, keepdims=True)))
        probs_low = reduced_copy(jnp.exp(masked - log_total))
        mixture = jnp.einsum('kgrc,ckd->rkgd', probs_low, value_span, precision=PRECISION_LEVEL)
        return mixture.reshape(BLOCK_TOKENS, QUERY_HEADS * HEAD_SIZE)
    result = lax.map(jax.checkpoint(one_block), (jnp.arange(count_of_blocks, dtype=jnp.int32), blocked_queries, position_blocks))
    return result.reshape(SEQUENCE_LENGTH, QUERY_HEADS * HEAD_SIZE)

def reference(inputs, positions, w_query, key_weight, value_weight, w_out, w_gate, w_up, w_down, gain_attn_in, gain_attn_out, gain_ffn_in, gain_ffn_out, cotangent):
    cos_part, sin_part = angles(positions, HEAD_SIZE)
    count_of_blocks = SEQUENCE_LENGTH // BLOCK_TOKENS
    contract_last = (((1,), (1,)), ((), ()))

    def forward_layer(residual, wq_full, gathered_key_weight, gathered_value_weight, wo_full, wg_full, wu_full, wd_full, gain_one, gain_two, gain_three, gain_four):
        attention_input = reduced_copy(normed(residual, gain_one))
        q_pre = reduced_backward(jnp.dot(attention_input, wq_full, precision=PRECISION_LEVEL)).reshape(SEQUENCE_LENGTH, QUERY_HEADS, HEAD_SIZE)
        query_values = reduced_copy(reduced_backward(rotate(q_pre, cos_part, sin_part)))
        key_before_rotary = reduced_backward(jnp.dot(attention_input, gathered_key_weight, precision=PRECISION_LEVEL)).reshape(SEQUENCE_LENGTH, KEY_VALUE_HEADS, HEAD_SIZE)
        key = reduced_copy(reduced_backward(rotate(key_before_rotary, cos_part, sin_part)))
        value_vectors = reduced_copy(reduced_backward(jnp.dot(attention_input, gathered_value_weight, precision=PRECISION_LEVEL))).reshape(SEQUENCE_LENGTH, KEY_VALUE_HEADS, HEAD_SIZE)
        attn = reduced_copy(reduced_backward(attend(query_values, key, value_vectors, positions)))
        branch = reduced_backward(lax.dot_general(attn, wo_full, contract_last, precision=PRECISION_LEVEL))
        mid = residual + normed(branch, gain_two)
        ffn_in = reduced_copy(normed(mid, gain_three))

        def unit_block(rows_in):
            gate_pre = reduced_backward(lax.dot_general(rows_in, wg_full, contract_last, precision=PRECISION_LEVEL))
            up_pre = reduced_backward(lax.dot_general(rows_in, wu_full, contract_last, precision=PRECISION_LEVEL))
            hidden = reduced_copy(gelu_tanh(gate_pre) * up_pre)
            return reduced_backward(jnp.dot(hidden, wd_full, precision=PRECISION_LEVEL))
        ffn_out = lax.map(jax.checkpoint(unit_block), ffn_in.reshape(count_of_blocks, BLOCK_TOKENS, MODEL_DIMENSION)).reshape(SEQUENCE_LENGTH, MODEL_DIMENSION)
        return mid + normed(ffn_out, gain_four)
    output, pullback = jax.vjp(forward_layer, inputs.astype(jnp.float32), w_query.astype(jnp.float32), key_weight.astype(jnp.float32), value_weight.astype(jnp.float32), w_out.astype(jnp.float32), w_gate.astype(jnp.float32), w_up.astype(jnp.float32), w_down.astype(jnp.float32), gain_attn_in, gain_attn_out, gain_ffn_in, gain_ffn_out)
    grads = pullback(cotangent.astype(jnp.float32))
    return (output, grads[0], grads[1], grads[2], grads[3], grads[4], grads[5], grads[6], grads[7], grads[8], grads[9], grads[10], grads[11])
```

```python
import functools
import math

import jax
import jax.numpy as jnp
from jax import lax
from jax.experimental import pallas as pl
from jax.experimental.pallas import tpu as pltpu
from jax.sharding import PartitionSpec as P

HEAD_SIZE = 256
WINDOW = 4096


NORM_EPS = 1e-06
SOFT_CAP = 50.0
UNIT_ROWS = 128
CHUNK_ROWS = 64
SHORT_CHUNK_ROWS = 32
GIVEN_ROWS = 96
EARLY_STEPS = 5
EARLY_UNITS = 2
GELU_SCALE = math.sqrt(2.0 / math.pi)
MESH = pl.DeviceIdType.MESH


def summed(array, axes):
    return lax.psum(array.astype(jnp.bfloat16), axes)


def after(arrays, others):
    return lax.optimization_barrier((tuple(arrays), tuple(others)))[0]


def normed(values, gain_vec):
    return (
        values
        * lax.rsqrt(jnp.mean(values * values, axis=-1, keepdims=True) + NORM_EPS)
        * (1.0 + gain_vec)
    )


def gelu_tanh(values):
    return jax.nn.gelu(values, approximate=True)


def angles(pos_rows, head_dim):
    frequency = jnp.exp(
        jnp.arange(head_dim // 2, dtype=jnp.float32) * (-2.0 * math.log(10000.0) / head_dim)
    )
    turned = pos_rows.astype(jnp.float32)[:, None] * frequency[None, :]
    return (jnp.cos(turned)[:, None, :], jnp.sin(turned)[:, None, :])


def rotate(values, cos_part, sin_part):
    half_dim = values.shape[-1] // 2
    first_half = values[..., :half_dim]
    second_half = values[..., half_dim:]
    return jnp.concatenate(
        [
            first_half * cos_part - second_half * sin_part,
            second_half * cos_part + first_half * sin_part,
        ],
        axis=-1,
    )


def rotate_back(values, cos_part, sin_part):
    half_dim = values.shape[-1] // 2
    first_half = values[..., :half_dim]
    second_half = values[..., half_dim:]
    return jnp.concatenate(
        [
            first_half * cos_part + second_half * sin_part,
            second_half * cos_part - first_half * sin_part,
        ],
        axis=-1,
    )


def dot_last(left_rows, right_rows):
    return lax.dot_general(
        left_rows, right_rows, (((1,), (1,)), ((), ())), preferred_element_type=jnp.float32
    )


def dot_first(left_rows, right_rows):
    return lax.dot_general(
        left_rows, right_rows, (((0,), (0,)), ((), ())), preferred_element_type=jnp.float32
    )


def gathered(array, axes):
    return lax.all_gather(array, axes, axis=0, tiled=True)


def scattered_low(array, axes):
    return lax.psum_scatter(array.astype(jnp.bfloat16), axes, scatter_dimension=0, tiled=True)


def scattered(array, axes):
    return scattered_low(array, axes).astype(jnp.float32)


def greet(partners):
    barrier = pltpu.get_barrier_semaphore()
    for partner in partners:
        pl.semaphore_signal(barrier, inc=1, device_id=partner, device_id_type=MESH)
    pl.semaphore_wait(barrier, len(partners))


class Cube:
    def __init__(self, dp_count, ctx_count):
        self.dp_count, self.ctx_count = dp_count, ctx_count
        count = dp_count * ctx_count
        self.far_bits = [
            1 << at for at in range(count.bit_length() - 1) if (1 << at) != ctx_count
        ]
        self.stages = len(self.far_bits)
        self.chips = 1 << self.stages

    def across(self, bit):
        dp, ctx = lax.axis_index("dp"), lax.axis_index("ctx")
        if bit < self.ctx_count:
            return dp, ctx + bit * (1 - 2 * lax.rem(ctx // bit, 2))
        bit = bit // self.ctx_count
        return dp + bit * (1 - 2 * lax.rem(dp // bit, 2)), ctx

    def device_across(self, bit):
        dp, ctx = self.across(bit)
        return {"dp": dp, "ctx": ctx}

    def sibling(self):
        dp, ctx = self.across(self.ctx_count)
        return {"dp": dp, "ctx": ctx}

    def far(self, stage):
        core = lax.rem(lax.axis_index("dp"), 2)
        dp0, ctx0 = self.across(self.far_bits[stage])
        dp1, ctx1 = self.across(self.far_bits[self.stages - 1 - stage])
        return {"dp": dp0 + core * (dp1 - dp0), "ctx": ctx0 + core * (ctx1 - ctx0)}

    def index(self):
        return lax.axis_index("dp") * self.ctx_count + lax.axis_index("ctx")

    def owner(self, block, half):
        index = self.index()
        core = lax.rem(lax.axis_index("dp"), 2)
        flipped = core + half - 2 * core * half

        def change(bit):
            return bit * (1 - 2 * lax.rem(index // bit, 2))

        owner = index + half * change(self.ctx_count)
        for stage in range(self.stages):
            change0 = change(self.far_bits[stage])
            change1 = change(self.far_bits[self.stages - 1 - stage])
            taken = lax.rem(block // (1 << stage), 2)
            owner = owner + taken * (change0 + flipped * (change1 - change0))
        return owner

    def partners(self):
        return [self.sibling()] + [self.far(stage) for stage in range(self.stages)]

    def greet(self):
        greet(self.partners())

    def stage_of(self, block):
        return block.bit_length() - 1

    def semaphores(self):
        per_block = pltpu.SemaphoreType.DMA((self.chips,))
        per_stage = pltpu.SemaphoreType.DMA((self.chips,))
        return [per_block, per_block, per_stage, per_stage] * 2


def remote(source, target, send_sem, recv_sem, device):
    return pltpu.make_async_remote_copy(
        src_ref=source,
        dst_ref=target,
        send_sem=send_sem,
        recv_sem=recv_sem,
        device_id=device,
        device_id_type=MESH,
    )


def gather_work_scatter(cube, own, whole, part, from_core, from_far, sems, arrived, work, partners=None, beside=None):
    core_send, core_recv, far_send, far_recv, back_send, back_recv, sum_send, sum_recv = sems
    stages, chips = cube.stages, cube.chips
    sibling = cube.sibling()
    fars = [cube.far(stage) for stage in range(stages)]

    def to_core(block):
        return remote(
            whole.at[block, 0], whole.at[block, 1], core_send.at[block], core_recv.at[block], sibling
        )

    def to_far(block, stage):
        at = block + (1 << stage)
        return remote(
            whole.at[block, 0], whole.at[at, 0], far_send.at[at], far_recv.at[at], fars[stage]
        )

    def sum_to_core(block):
        return remote(
            part.at[block, 1], from_core.at[block], back_send.at[block], back_recv.at[block], sibling
        )

    def sum_to_far(block):
        stage = cube.stage_of(block)
        return remote(
            part.at[block, 0], from_far.at[block], sum_send.at[block], sum_recv.at[block], fars[stage]
        )

    def fold(block):
        sum_to_core(block).wait_recv()
        part[block, 0] = (
            part[block, 0].astype(jnp.float32) + from_core[block].astype(jnp.float32)
        ).astype(jnp.bfloat16)
        if stages and block >= chips // 2:
            sum_to_far(block).start()

    def relay():
        for stage in reversed(range(stages)):
            for block in reversed(range(1, 1 << stage)):
                slot = block + (1 << stage)
                sum_to_far(slot).wait_recv()
                part[block, 0] = (
                    part[block, 0].astype(jnp.float32) + from_far[slot].astype(jnp.float32)
                ).astype(jnp.bfloat16)
                if cube.stage_of(block) == stage - 1:
                    sum_to_far(block).start()

    beside = beside or (lambda point: None)
    greet(partners or cube.partners())
    whole[0, 0] = own[...]
    if stages:
        to_far(0, 0).start()
    to_core(0).start()
    for block in [*range(1, chips), 0]:
        if block:
            stage = cube.stage_of(block)
            to_far(block - (1 << stage), stage).wait_recv()
            if block == 1:
                for later in range(1, stages):
                    to_far(0, later).start()
            for later in range(stage + 1, stages):
                to_far(block, later).start()
            to_core(block).start()
            to_core(block).wait_recv()
        if block == 1:
            to_core(0).wait_recv()
        arrived(block)
        if block == chips - 1:
            beside(0)
        if not block and chips > 1:
            fold(chips - 1)
            beside(1)
        between = functools.partial(fold, block - 1) if block > 1 else None
        work(block, between if block else relay)
        sum_to_core(block).start()
    beside(2)
    sum_to_core(0).wait_recv()
    total = part[0, 0].astype(jnp.float32) + from_core[0].astype(jnp.float32)
    for stage in reversed(range(stages)):
        sum_to_far(1 << stage).wait_recv()
        total = total + from_far[1 << stage].astype(jnp.float32)
    for block in range(chips):
        to_core(block).wait_send()
        sum_to_core(block).wait_send()
        if block:
            stage = cube.stage_of(block)
            to_far(block - (1 << stage), stage).wait_send()
            sum_to_far(block).wait_send()
    return total


def tiles_of(width, most):
    tile = max(size for size in range(128, most + 1, 128) if width % size == 0)
    return [pl.ds(first, tile) for first in range(0, width, tile)]


def ffn_forward_kernel(
    cube, own, w_gate, w_up, w_down, out, whole_out, hidden_out, act_out, slope_out,
    whole, gate_rows, up_rows, down_rows, hidden, act, slope, part, from_core, from_far,
    load, save, *sems,
):
    chips = cube.chips
    units, width = gate_rows.shape
    rows = 2 * own.shape[0]
    loads = [
        pltpu.make_async_copy(source, target, load.at[at])
        for at, (source, target) in enumerate(
            [(w_gate, gate_rows), (w_up, up_rows), (w_down, down_rows)]
        )
    ]
    for copy in loads:
        copy.start()

    kept = [(whole, whole_out), (hidden, hidden_out), (act, act_out), (slope, slope_out)]

    def saved(kind, block):
        source, target = kept[kind]
        return pltpu.make_async_copy(source.at[block], target.at[block], save.at[kind, block])

    def arrived(block):
        saved(0, block).start()

    def work(block, between):
        if block == 1:
            loads[0].wait()
            loads[1].wait()
        tokens = whole[block].reshape(rows, width)
        for tile in tiles_of(units, 384):
            gate = dot_last(tokens, gate_rows[tile, :])
            up = dot_last(tokens, up_rows[tile, :])
            square = gate * gate
            bent = jnp.tanh(GELU_SCALE * gate * (1.0 + 0.044715 * square))
            half = 0.5 + 0.5 * bent
            active = gate * half
            steep = half + (0.5 * GELU_SCALE) * gate * (1.0 - bent * bent) * (
                1.0 + (3 * 0.044715) * square
            )
            hidden[block, :, tile] = (active * up).astype(jnp.bfloat16)
            act[block, :, tile] = active.astype(jnp.bfloat16)
            slope[block, :, tile] = (up * steep).astype(jnp.bfloat16)
        if block == 1:
            loads[2].wait()
        units_now = hidden[block]
        for tile in tiles_of(width, 768):
            sums = jnp.dot(units_now, down_rows[:, tile], preferred_element_type=jnp.float32)
            part[block, :, :, tile] = sums.astype(jnp.bfloat16).reshape(2, rows // 2, tile.size)
        for kind in range(1, len(kept)):
            saved(kind, block).start()
        if between:
            between()

    out[...] = gather_work_scatter(
        cube, own, whole, part, from_core, from_far, sems, arrived, work
    )
    for block in range(chips):
        for kind in range(len(kept)):
            saved(kind, block).wait()


def ffn_backward_kernel(
    cube, own, w_gate, w_up, w_down, act_in, slope_in, hidden_in, out, whole_out, gate_out, up_out,
    early_out, whole, gate_rows, up_rows, down_rows, act, slope, part, from_core, from_far,
    load, save, hidden, line_own, from_end, from_middle, line_sems, *sems,
):
    chips = cube.chips
    units, width = gate_rows.shape
    rows = 2 * own.shape[0]
    loads = [
        pltpu.make_async_copy(source, target, load.at[at])
        for at, (source, target) in enumerate(
            [
                (w_down, down_rows),
                (act_in, act),
                (slope_in, slope),
                (w_gate, gate_rows),
                (w_up, up_rows),
                (hidden_in.at[:, :, pl.ds(0, hidden.shape[2])], hidden),
            ]
        )
    ]
    for copy in loads:
        copy.start()

    kept = [(whole, whole_out), (slope, gate_out), (act, up_out)]

    def saved(kind, block):
        source, target = kept[kind]
        return pltpu.make_async_copy(source.at[block], target.at[block], save.at[kind, block])

    def arrived(block):
        saved(0, block).start()

    def work(block, between):
        if block == 1:
            for copy in loads[:3]:
                copy.wait()
        grads = whole[block].reshape(rows, width)
        for tile in tiles_of(units, 384):
            grad_hidden = dot_last(grads, down_rows[tile, :])
            slope[block, :, tile] = (
                grad_hidden * slope[block, :, tile].astype(jnp.float32)
            ).astype(jnp.bfloat16)
            act[block, :, tile] = (grad_hidden * act[block, :, tile].astype(jnp.float32)).astype(
                jnp.bfloat16
            )
        if block == 1:
            for copy in loads[3:]:
                copy.wait()
        if between:
            between()
        grad_gate, grad_up = slope[block], act[block]
        for tile in tiles_of(width, 768):
            sums = jnp.dot(grad_gate, gate_rows[:, tile], preferred_element_type=jnp.float32)
            sums = sums + jnp.dot(grad_up, up_rows[:, tile], preferred_element_type=jnp.float32)
            part[block, :, :, tile] = sums.astype(jnp.bfloat16).reshape(2, rows // 2, tile.size)
        for kind in range(1, len(kept)):
            saved(kind, block).start()

    line = Line()
    job = LineJob(line, line_own, from_end, from_middle, from_end, early_out, line_sems)
    per_unit = job.depth = UNIT_ROWS // line_own.shape[1]

    def beside(point):
        chunks = range(point * per_unit, (point + 1) * per_unit)
        if point < EARLY_UNITS:
            unit_product(hidden, whole, line_own, point)

            @pl.when(line.is_end)
            def _():
                for at in chunks:
                    job.send_end(jnp.int32(at))

        if point:

            @pl.when(jnp.logical_not(line.is_end))
            def _():
                for at in chunks:
                    job.add_middle(jnp.int32(at - per_unit))
                if point == EARLY_UNITS:
                    job.finish_middle(job.count - 1)

    out[...] = gather_work_scatter(
        cube,
        own,
        whole,
        part,
        from_core,
        from_far,
        sems,
        arrived,
        work,
        cube.partners() + [{"seq": lax.rem(line.place + ahead, 4)} for ahead in range(1, 4)],
        beside,
    )

    @pl.when(line.is_end)
    def _():
        job.close_end()

    @pl.when(jnp.logical_not(line.is_end))
    def _():
        job.close_middle()

    for block in range(chips):
        for kind in range(len(kept)):
            saved(kind, block).wait()


def cube_fits(dp_count, ctx_count, tok_rows, units, width):
    count = dp_count * ctx_count
    if count & (count - 1) or dp_count % 2:
        return False
    tokens = count * tok_rows
    held = 2 * (5 * tokens * width // 2 + 3 * units * width + 3 * tokens * units)
    return held <= 48 * 2**20 and tok_rows % 16 == 0


def ffn_call(kernel, cube, collective_id, own, weights, extras, kept, early=()):
    tok_rows, width = own.shape
    units = weights[0].shape[0]
    chips = cube.chips
    rows = 2 * tok_rows
    low = jnp.bfloat16
    unit_block = (chips, rows, units)
    inside = pl.BlockSpec(memory_space=pltpu.VMEM)
    outside = pl.BlockSpec(memory_space=pl.ANY)
    chunks = (EARLY_UNITS * UNIT_ROWS // SHORT_CHUNK_ROWS, SHORT_CHUNK_ROWS, width)
    line_scratch = [
        pltpu.VMEM((chips, rows, EARLY_UNITS * UNIT_ROWS), low),
        pltpu.VMEM(chunks, low),
        pltpu.VMEM(chunks, low),
        pltpu.VMEM(chunks, low),
        pltpu.SemaphoreType.DMA((7, chunks[0])),
    ]
    return pl.pallas_call(
        functools.partial(kernel, cube),
        out_shape=[
            jax.ShapeDtypeStruct((tok_rows, width), jnp.float32),
            jax.ShapeDtypeStruct((chips, 2, tok_rows, width), low),
        ]
        + [jax.ShapeDtypeStruct(unit_block, low)] * kept
        + [jax.ShapeDtypeStruct(chunks, low)] * len(early),
        in_specs=[inside] + [outside] * (3 + len(extras) + len(early)),
        out_specs=[inside] + [outside] * (1 + kept + len(early)),
        scratch_shapes=[pltpu.VMEM((chips, 2, tok_rows, width), low)]
        + [pltpu.VMEM((units, width), low)] * 3
        + [pltpu.VMEM(unit_block, low)] * max(kept, len(extras))
        + [
            pltpu.VMEM((chips, 2, tok_rows, width), low),
            pltpu.VMEM((chips, tok_rows, width), low),
            pltpu.VMEM((chips, tok_rows, width), low),
            pltpu.SemaphoreType.DMA((3 + len(extras) + len(early),)),
            pltpu.SemaphoreType.DMA((1 + kept, chips)),
        ]
        + line_scratch * len(early)
        + cube.semaphores(),
        compiler_params=pltpu.CompilerParams(
            collective_id=collective_id,
            has_side_effects=True,
            vmem_limit_bytes=60 * 2**20,
        ),
        cost_estimate=pl.CostEstimate(
            flops=6 * chips * rows * units * width,
            bytes_accessed=6 * units * width + 6 * chips * rows * units,
            transcendentals=0,
        ),
    )(own, *weights, *extras, *early)


class Line:
    def __init__(self):
        self.place = lax.axis_index("seq")
        self.is_end = (self.place == 0) | (self.place == 3)
        low = self.place // 2
        self.end = {"seq": 3 * low}
        self.middle = {"seq": 1 + low}
        self.other_middle = {"seq": 2 - low}


class LineJob:
    def __init__(self, line, own, from_end, from_middle, total, out, sems):
        self.line = line
        self.own, self.from_end, self.from_middle = own, from_end, from_middle
        self.total, self.out, self.sems = total, out, sems
        self.count = own.shape[0]
        self.before = None
        self.first = 0
        self.depth = 2

    def inward(self, at):
        sems = self.sems
        return remote(
            self.own.at[at], self.from_end.at[at], sems.at[0, at], sems.at[1, at], self.line.middle
        )

    def across(self, at):
        sems = self.sems
        return remote(
            self.own.at[at],
            self.from_middle.at[at],
            sems.at[2, at],
            sems.at[3, at],
            self.line.other_middle,
        )

    def outward(self, at):
        sems = self.sems
        return remote(
            self.total.at[at], self.total.at[at], sems.at[4, at], sems.at[5, at], self.line.end
        )

    def save(self, at):
        return pltpu.make_async_copy(
            self.total.at[at], self.out.at[at + self.first], self.sems.at[6, at]
        )

    def send_end(self, at):
        @pl.when(at >= self.depth)
        def _():
            self.inward(at - self.depth).wait_send()

        self.inward(at).start()

    def add_middle(self, at):
        self.inward(at).wait_recv()
        self.own[at] = (
            self.own[at].astype(jnp.float32) + self.from_end[at].astype(jnp.float32)
        ).astype(jnp.bfloat16)
        self.across(at).start()

        @pl.when(at >= 1)
        def _():
            self.finish_middle(at - 1)

        if self.before:

            @pl.when(at == 0)
            def _():
                self.before.finish_middle(self.before.count - 1)

    def finish_middle(self, at):
        self.across(at).wait_recv()
        self.total[at] = (
            self.own[at].astype(jnp.float32) + self.from_middle[at].astype(jnp.float32)
        ).astype(jnp.bfloat16)
        self.outward(at).start()
        self.save(at).start()

    def each(self, body):
        def step(at, carry):
            body(at)
            return carry

        lax.fori_loop(0, self.count, step, 0)

    def close_end(self):
        def body(at):
            self.outward(at).wait_recv()
            self.save(at).start()

        self.each(body)
        self.each(lambda at: self.save(at).wait())
        for at in range(max(self.count - self.depth, 0), self.count):
            self.inward(at).wait_send()

    def close_middle(self):
        def body(at):
            self.across(at).wait_send()
            self.outward(at).wait_send()
            self.save(at).wait()

        self.each(body)


class Spread:
    def __init__(self, line, block, slots, sems, out=None, shares=(), save=None):
        self.place, self.block, self.slots, self.sems = line.place, block, slots, sems
        self.out, self.shares, self.save = out, shares, save

    def hop(self, way, turn, slot):
        sems = self.sems
        at = 0 if way > 0 else 2
        return remote(
            self.slots.at[slot],
            self.slots.at[slot],
            sems.at[at, turn],
            sems.at[at + 1, turn],
            {"seq": self.place + way},
        )

    def each(self, turn, held, body):
        for way in (1, -1):
            slot = self.place - way * (turn if held else turn + 1)
            near = self.place + way if held else self.place - way
            inside = (slot >= 0) & (slot <= 3) & (near >= 0) & (near <= 3)

            @pl.when(inside)
            def _(way=way, slot=slot):
                body(self.hop(way, turn, slot) if held else self.arrival(way, turn, slot))

    def arrival(self, way, turn, slot):
        at = 0 if way > 0 else 2
        return remote(
            self.slots.at[slot],
            self.slots.at[slot],
            self.sems.at[at, turn],
            self.sems.at[at + 1, turn],
            {"seq": self.place - way},
        )

    def start(self):
        self.slots[self.place] = self.block[...]
        self.each(0, True, lambda copy: copy.start())

    def forward_turn(self, turn):
        self.each(turn - 1, False, lambda copy: copy.wait_recv())
        if turn <= 2:
            self.each(turn, True, lambda copy: copy.start())

    def forward(self):
        self.forward_turn(1)
        self.forward_turn(2)

    def close_sends(self):
        for turn in range(3):
            self.each(turn, True, lambda copy: copy.wait_send())

    def close(self):
        self.forward_turn(3)
        if self.out is None:
            self.close_sends()
            return
        saves, first = [], 0
        for share in self.shares:
            for slot in range(4):
                source = self.slots.at[slot, :, pl.ds(first, share)]
                target = self.out.at[:, pl.ds(4 * first + slot * share, share)]
                saves.append(pltpu.make_async_copy(source, target, self.save.at[len(saves)]))
            first += share
        for save in saves:
            save.start()
        self.close_sends()
        for save in saves:
            save.wait()


class Swap:
    def __init__(self, blocks, landed, send_sems, recv_sems):
        self.blocks, self.landed = blocks, landed
        self.send_sems, self.recv_sems = send_sems, recv_sems
        self.count = blocks.shape[0]
        self.place = lax.axis_index("seq")

    def peer(self, ahead):
        return lax.rem(self.place + ahead, self.count)

    def copy(self, ahead, slot):
        peer = self.peer(ahead)
        return remote(
            self.blocks.at[peer],
            self.landed.at[slot],
            self.send_sems.at[ahead],
            self.recv_sems.at[ahead],
            {"seq": peer},
        )

    def start(self, ahead):
        self.copy(ahead, self.place).start()

    def keep(self):
        self.landed[self.place] = self.blocks[self.place]

    def wait_recv(self):
        for ahead in range(1, self.count):
            self.copy(ahead, self.peer(self.count - ahead)).wait_recv()

    def wait_send(self):
        for ahead in range(1, self.count):
            self.copy(ahead, self.place).wait_send()

    def others(self):
        return [{"seq": self.peer(ahead)} for ahead in range(1, self.count)]


class CubeGather:
    def __init__(self, cube, whole, sems):
        self.cube, self.whole = cube, whole
        self.core_send, self.core_recv, self.far_send, self.far_recv = sems
        self.sibling = cube.sibling()
        self.fars = [cube.far(stage) for stage in range(cube.stages)]

    def to_core(self, block):
        at = self.whole.at[self.cube.owner(block, 0)]
        return remote(at, at, self.core_send.at[block], self.core_recv.at[block], self.sibling)

    def from_core(self, block):
        at = self.whole.at[self.cube.owner(block, 1)]
        return remote(at, at, self.core_send.at[block], self.core_recv.at[block], self.sibling)

    def to_far(self, block, stage):
        slot = block + (1 << stage)
        at = self.whole.at[self.cube.owner(block, 0)]
        return remote(at, at, self.far_send.at[slot], self.far_recv.at[slot], self.fars[stage])

    def from_far(self, slot):
        stage = self.cube.stage_of(slot)
        at = self.whole.at[self.cube.owner(slot, 0)]
        return remote(at, at, self.far_send.at[slot], self.far_recv.at[slot], self.fars[stage])

    def start(self):
        self.to_far(0, 0).start()
        self.to_core(0).start()

    def step(self, block):
        if block:
            self.from_far(block).wait_recv()
            if block == 1:
                for later in range(1, self.cube.stages):
                    self.to_far(0, later).start()
            for later in range(self.cube.stage_of(block) + 1, self.cube.stages):
                self.to_far(block, later).start()
            self.to_core(block).start()

    def step_core(self, block):
        self.from_core(block).wait_recv()

    def close(self):
        for block in range(self.cube.chips):
            self.to_core(block).wait_send()
            if block:
                stage = self.cube.stage_of(block)
                self.to_far(block - (1 << stage), stage).wait_send()


def front_kernel(
    cube, own, gain, cosine, sine, lower, w_query, key_weight, value_weight,
    attn_in_out, weights_out, query_out, pairs_out, mixture_out, log_out, tokens_out,
    slots, attn_in, weights, pairs, sums, heads_low, tokens,
    spread_sems, save, token_send, token_recv, *cube_sems,
):
    count, tok_rows, model_width = slots.shape
    rows, q_width = query_out.shape
    heads = q_width // HEAD_SIZE
    half_size = HEAD_SIZE // 2
    me = cube.index()
    place = lax.axis_index("seq")
    line = Line()
    spread = Spread(line, own, slots, spread_sems)
    weight_gather = CubeGather(cube, weights, cube_sems[:4])
    pair_gather = CubeGather(cube, pairs, cube_sems[4:])
    swap = Swap(heads_low, tokens, token_send, token_recv)
    cuts, first = [], 0
    for weight, share in ((w_query, q_width), (key_weight, HEAD_SIZE), (value_weight, HEAD_SIZE)):
        cuts.append(
            pltpu.make_async_copy(
                weight.at[:, pl.ds(pl.multiple_of(place * share, share), share)],
                weights.at[me, :, pl.ds(first, share)],
                save.at[3 + len(cuts)],
            )
        )
        first += share
    for cut in cuts:
        cut.start()
    greet(cube.partners() + swap.others())

    spread.start()
    for cut in cuts:
        cut.wait()
    weight_gather.start()

    def prepare(slot):
        values = slots[slot].astype(jnp.float32)
        scale = lax.rsqrt(jnp.mean(values * values, axis=-1, keepdims=True) + NORM_EPS)
        attn_in[slot] = (values * scale * (1.0 + gain[...])).astype(jnp.bfloat16)

    def project(slot):
        here = pl.ds(pl.multiple_of(slot * tok_rows, tok_rows), tok_rows)
        cos_part, sin_part = cosine[slot], sine[slot]
        tokens_now = attn_in[slot]

        def turned(first):
            columns = pl.ds(first, HEAD_SIZE)
            values = jnp.dot(
                tokens_now,
                weights[:, :, columns].reshape(model_width, HEAD_SIZE),
                preferred_element_type=jnp.float32,
            )
            left, right = values[:, :half_size], values[:, half_size:]
            return values, jnp.concatenate(
                [left * cos_part - right * sin_part, right * cos_part + left * sin_part], axis=-1
            ).astype(jnp.bfloat16)

        for head in range(heads):
            query_out[here, pl.ds(head * HEAD_SIZE, HEAD_SIZE)] = turned(head * HEAD_SIZE)[1]
        pairs[me, here, :HEAD_SIZE] = turned(q_width)[1]
        pairs[me, here, HEAD_SIZE:] = turned(q_width + HEAD_SIZE)[0].astype(jnp.bfloat16)

    def arrivals(turn, body):
        for way in (1, -1):
            slot = place - way * (turn + 1)

            @pl.when((slot >= 0) & (slot < count))
            def _(slot=slot):
                body(slot)

    prepare(place)
    for block in range(cube.chips // 2):
        weight_gather.step(block)
    spread.forward_turn(1)
    arrivals(0, prepare)
    for block in range(cube.chips // 2, cube.chips):
        weight_gather.step(block)
    for block in range(cube.chips):
        weight_gather.step_core(block)
    save_weights = pltpu.make_async_copy(weights, weights_out, save.at[0])
    save_weights.start()
    project(place)
    arrivals(0, project)
    spread.forward_turn(2)
    arrivals(1, prepare)
    arrivals(1, project)
    spread.forward_turn(3)
    arrivals(2, prepare)
    arrivals(2, project)
    save_attn_in = pltpu.make_async_copy(attn_in, attn_in_out, save.at[1])
    save_attn_in.start()
    pair_gather.start()

    mixture_out[...] = jnp.zeros_like(mixture_out)
    sums[...] = jnp.zeros_like(sums)
    tall = rows // 2

    def attend(owner, head, first):
        columns = pl.ds(pl.multiple_of(head * HEAD_SIZE, HEAD_SIZE), HEAD_SIZE)
        key, value = pairs[owner, :, :HEAD_SIZE], pairs[owner, :, HEAD_SIZE:]
        key_ids = owner * rows + lax.broadcasted_iota(jnp.int32, (1, rows), 1)
        here = pl.ds(first, tall)
        raw = dot_last(query_out[here, columns], key)
        capped = SOFT_CAP * jnp.tanh(raw * (HEAD_SIZE ** (-0.5) / SOFT_CAP))
        row_ids = me * rows + first + lax.broadcasted_iota(jnp.int32, (tall, 1), 0)
        allowed = (key_ids <= row_ids) & (key_ids >= lower[here, :])
        weight = jnp.where(allowed, jnp.exp(capped), 0.0)
        sums[head, here, :] += jnp.sum(weight, axis=-1, keepdims=True)
        mixture_out[here, columns] += jnp.dot(
            weight.astype(jnp.bfloat16), value, preferred_element_type=jnp.float32
        )

    def attend_owner(block, half, firsts):
        owner = cube.owner(block, half)

        @pl.when(owner <= me)
        def _():
            def step(head, carry):
                for first in firsts:
                    attend(owner, head, first)
                return carry

            lax.fori_loop(0, heads, step, 0)

    def finish(first):
        here = pl.ds(first, tall)
        blocks = pl.ds(first // tok_rows, tall // tok_rows)
        for head in range(heads):
            columns = pl.ds(head * HEAD_SIZE, HEAD_SIZE)
            mixed = mixture_out[here, columns] / sums[head, here, :]
            mixture_out[here, columns] = mixed
            heads_low[blocks, :, columns] = mixed.astype(jnp.bfloat16).reshape(
                tall // tok_rows, tok_rows, HEAD_SIZE
            )
            log_out[head, here, :] = jnp.log(sums[head, here, :])
        for ahead in range(1, count):

            @pl.when(swap.peer(ahead) // (tall // tok_rows) == first // tall)
            def _(ahead=ahead):
                swap.start(ahead)

    final = cube.chips - 1
    firsts = range(0, rows, tall)
    for block in range(final):
        pair_gather.step(block)
        attend_owner(block, 0, firsts)
        pair_gather.step_core(block)
        attend_owner(block, 1, firsts)
    pair_gather.step(final)
    for first in firsts:
        attend_owner(final, 0, [first])
        if not first:
            pair_gather.step_core(final)
        attend_owner(final, 1, [first])
        finish(first)
    save_pairs = pltpu.make_async_copy(pairs, pairs_out, save.at[2])
    save_pairs.start()
    swap.keep()
    pair_gather.close()
    weight_gather.close()
    spread.close_sends()
    swap.wait_recv()
    for other in range(count):
        tokens_out[:, pl.ds(other * q_width, q_width)] = tokens[other]
    swap.wait_send()
    save_weights.wait()
    save_attn_in.wait()
    save_pairs.wait()


def front(cube, collective_id, own, projections, gain, cosine, sine, lower):
    count = 4
    tok_rows, width = own.shape
    weight_rows = projections[0].shape[0]
    head_columns = sum(weight.shape[1] for weight in projections) // count
    layer_count = 2 * cube.chips
    rows = count * tok_rows
    q_width = head_columns - 2 * HEAD_SIZE
    heads = q_width // HEAD_SIZE
    low, full = jnp.bfloat16, jnp.float32
    inside = pl.BlockSpec(memory_space=pltpu.VMEM)
    outside = pl.BlockSpec(memory_space=pl.ANY)
    attn_in, weights, query, pairs, mixture, log_total, tokens = pl.pallas_call(
        functools.partial(front_kernel, cube),
        out_shape=[
            jax.ShapeDtypeStruct((count, tok_rows, width), low),
            jax.ShapeDtypeStruct((layer_count, weight_rows, head_columns), low),
            jax.ShapeDtypeStruct((rows, q_width), low),
            jax.ShapeDtypeStruct((layer_count, rows, 2 * HEAD_SIZE), low),
            jax.ShapeDtypeStruct((rows, q_width), full),
            jax.ShapeDtypeStruct((heads, rows, 1), full),
            jax.ShapeDtypeStruct((tok_rows, count * q_width), low),
        ],
        in_specs=[inside] * 5 + [outside] * 3,
        out_specs=[outside, outside, inside, outside, inside, inside, inside],
        scratch_shapes=[
            pltpu.VMEM((count, tok_rows, width), low),
            pltpu.VMEM((count, tok_rows, width), low),
            pltpu.VMEM((layer_count, weight_rows, head_columns), low),
            pltpu.VMEM((layer_count, rows, 2 * HEAD_SIZE), low),
            pltpu.VMEM((heads, rows, 1), full),
            pltpu.VMEM((count, tok_rows, q_width), low),
            pltpu.VMEM((count, tok_rows, q_width), low),
            pltpu.SemaphoreType.DMA((4, 3)),
            pltpu.SemaphoreType.DMA((6,)),
            pltpu.SemaphoreType.DMA((count,)),
            pltpu.SemaphoreType.DMA((count,)),
        ]
        + cube.semaphores(),
        compiler_params=pltpu.CompilerParams(
            collective_id=collective_id,
            has_side_effects=True,
            vmem_limit_bytes=60 * 2**20,
        ),
        cost_estimate=pl.CostEstimate(
            flops=16 * rows * rows * layer_count * q_width,
            bytes_accessed=0,
            transcendentals=0,
        ),
    )(
        own,
        gain.reshape(1, width),
        cosine,
        sine,
        lower.reshape(rows, 1),
        *projections,
    )
    return (
        attn_in.reshape(rows, width),
        weights.reshape(-1, head_columns),
        query,
        pairs.reshape(-1, 2 * HEAD_SIZE),
        mixture,
        log_total.reshape(heads, rows),
        tokens,
    )


def unit_product(left, right, own, unit, skip=0):
    chunk_rows, width = own.shape[1:]
    per_unit = UNIT_ROWS // chunk_rows
    columns = pl.ds(pl.multiple_of((unit + skip) * UNIT_ROWS, UNIT_ROWS), UNIT_ROWS)

    def columns_of(ref, columns):
        values = ref[(slice(None),) * (len(ref.shape) - 1) + (columns,)]
        return values.reshape(-1, values.shape[-1])

    flipped = columns_of(left, columns).T
    for tile in tiles_of(width, 768):
        sums = jnp.dot(flipped, columns_of(right, tile), preferred_element_type=jnp.float32)
        own[pl.ds(unit * per_unit, per_unit), :, tile] = sums.astype(jnp.bfloat16).reshape(
            per_unit, chunk_rows, tile.size
        )


def norm_backward(values, gain, grad):
    scale = lax.rsqrt(jnp.mean(values * values, axis=-1, keepdims=True) + NORM_EPS)
    gained = (1.0 + gain) * grad
    back = scale * gained - values * (
        scale * scale * scale * jnp.mean(values * gained, axis=-1, keepdims=True)
    )
    return back, jnp.sum(values * scale * grad, axis=0, keepdims=True)


def attention_backward_kernel(
    cube, grad_model, mid, branch, cotangent, gain_in, gain_out, mixture, query, log_total, lower,
    tokens, cosine, sine, w_out, pairs_in, left_in, right_in, attn_in, early,
    mid_out, gains_out, grads_out, out_part, column_part, total_out,
    branch_low, wide, left, right, part, from_core, from_far, query_sums, pair_sums, delta, to_heads, heads_in,
    own, from_end, from_middle, line_sems, loads, saves, swap_send, swap_recv,
    back_send, back_recv, sum_send, sum_recv,
):
    rows, width = query.shape
    count, tok_rows, _ = to_heads.shape
    model_width = mid.shape[1]
    heads = width // HEAD_SIZE
    stages, chips = cube.stages, cube.chips
    top = stages - 1
    me = cube.index()
    sibling = cube.sibling()
    fars = [cube.far(stage) for stage in range(stages)]
    line = Line()
    job = LineJob(line, own, from_end, from_middle, from_end, total_out, line_sems)
    job.first = early.shape[0]
    per_unit = UNIT_ROWS // own.shape[1]
    skip = early.shape[0] // per_unit
    swap = Swap(to_heads, heads_in, swap_send, swap_recv)
    row_ids = me * rows + lax.broadcasted_iota(jnp.int32, (1, rows), 1)
    tall = rows // 2
    pair_rows = pairs_in.shape[0]
    load_left = pltpu.make_async_copy(left_in, left, loads.at[0])
    load_right = pltpu.make_async_copy(right_in, right, loads.at[1])
    load_pairs = pltpu.make_async_copy(pairs_in, wide.at[pl.ds(0, pair_rows)], loads.at[2])
    load_out = [
        pltpu.make_async_copy(
            w_out.at[:, pl.ds(block * width, width)],
            wide.at[pl.ds(block * model_width, model_width)],
            loads.at[3 + block],
        )
        for block in range(count)
    ]
    load_attn_in = pltpu.make_async_copy(attn_in, right.at[pl.ds(0, rows)], loads.at[3 + count])

    def saved(target, block, at):
        return pltpu.make_async_copy(
            wide.at[pl.ds(block * model_width, model_width)],
            target.at[:, pl.ds(block * width, width)],
            saves.at[at],
        )

    save_out = [saved(out_part, block, block) for block in range(count)]
    save_columns = [saved(column_part, block, count + block) for block in range(2)]
    move_early = pltpu.make_async_copy(
        early, total_out.at[pl.ds(0, job.first)], loads.at[4 + count]
    )
    load_left.start()
    load_right.start()
    for copy in load_out:
        copy.start()
    move_early.start()

    def sum_to_core(block):
        return remote(
            part.at[block, 1], from_core.at[block], back_send.at[block], back_recv.at[block], sibling
        )

    def sum_to_far(block, stage):
        return remote(
            part.at[block, 0], from_far.at[block], sum_send.at[block], sum_recv.at[block], fars[stage]
        )

    def one_head(owner, head):
        columns = pl.ds(head * HEAD_SIZE, HEAD_SIZE)
        query_head = query[:, columns]
        grad_head = heads_in[:, :, columns].reshape(rows, HEAD_SIZE)
        log_head, delta_head = log_total[head : head + 1, :], delta[head : head + 1, :]
        for first in range(0, rows, tall):
            here = pl.ds(pl.multiple_of(owner * rows, rows) + first, tall)
            key, value = wide[here, :HEAD_SIZE], wide[here, HEAD_SIZE:]
            bent = jnp.tanh(dot_last(key, query_head) * (HEAD_SIZE ** (-0.5) / SOFT_CAP))
            key_ids = owner * rows + first + lax.broadcasted_iota(jnp.int32, (tall, 1), 0)
            allowed = (key_ids <= row_ids) & (key_ids >= lower[...])
            probs = jnp.where(allowed, jnp.exp(SOFT_CAP * bent - log_head), 0.0)
            grad_raw = (
                probs
                * (dot_last(value, grad_head) - delta_head)
                * ((1.0 - bent * bent) * HEAD_SIZE ** (-0.5))
            ).astype(jnp.bfloat16)
            key_sums = jnp.dot(grad_raw, query_head, preferred_element_type=jnp.float32)
            value_sums = jnp.dot(
                probs.astype(jnp.bfloat16), grad_head, preferred_element_type=jnp.float32
            )
            inner = pl.ds(first, tall)
            if head:
                key_sums = key_sums + pair_sums[inner, :HEAD_SIZE]
                value_sums = value_sums + pair_sums[inner, HEAD_SIZE:]
            pair_sums[inner, :HEAD_SIZE] = key_sums
            pair_sums[inner, HEAD_SIZE:] = value_sums
            query_sums[:, columns] += dot_first(grad_raw, key)

    def line_step(at):
        @pl.when(at < job.count)
        def _():
            @pl.when(lax.rem(at, per_unit) == 0)
            def _():
                unit_product(left, right, own, at // per_unit, skip)

            @pl.when(line.is_end)
            def _():
                job.send_end(at)

            @pl.when(jnp.logical_not(line.is_end) & (at >= 1))
            def _():
                job.add_middle(at - 1)

    def turn(step, carry):
        block = chips - 1 - step // 2
        half = 1 - lax.rem(step, 2)
        owner = cube.owner(block, half)

        @pl.when(owner <= me)
        def _():
            for head in range(heads):
                one_head(owner, head)
            part[block, half] = pair_sums[...].astype(jnp.bfloat16)

        @pl.when(owner > me)
        def _():
            part[block, half] = jnp.zeros_like(part[block, half])

        @pl.when(half == 1)
        def _():
            sum_to_core(block).start()

        @pl.when(half == 0)
        def _():
            sum_to_core(block).wait_recv()
            part[block, 0] = (
                part[block, 0].astype(jnp.float32) + from_core[block].astype(jnp.float32)
            ).astype(jnp.bfloat16)

            @pl.when(block >= chips // 2)
            def _():
                sum_to_far(block, top).start()

        line_step(EARLY_STEPS + step)

        @pl.when(step == 2 * chips - 3)
        def _():
            for stage in reversed(range(1, stages)):
                for block in reversed(range(1, 1 << stage)):
                    slot = block + (1 << stage)
                    sum_to_far(slot, stage).wait_recv()
                    part[block, 0] = (
                        part[block, 0].astype(jnp.float32) + from_far[slot].astype(jnp.float32)
                    ).astype(jnp.bfloat16)
                    if cube.stage_of(block) == stage - 1:
                        sum_to_far(block, stage - 1).start()

        return carry

    greet(cube.partners() + swap.others())
    load_left.wait()
    load_right.wait()
    line_step(jnp.int32(0))

    grad_mid, gain_sum = norm_backward(mid[...], gain_in[...], grad_model[...])
    grad_mid = cotangent[...].astype(jnp.float32) + grad_mid
    mid_out[...] = grad_mid
    gains_out[0:1, :] = gain_sum
    grad_branch, gain_sum = norm_backward(branch[...], gain_out[...], grad_mid)
    gains_out[1:2, :] = gain_sum
    branch_low[...] = grad_branch.astype(jnp.bfloat16)
    line_step(jnp.int32(1))
    for copy in load_out:
        copy.wait()
    for ahead in [*range(1, count), 0]:
        peer = swap.peer(ahead)
        here = pl.ds(pl.multiple_of(peer * model_width, model_width), model_width)
        to_heads[peer] = jnp.dot(
            branch_low[...], wide[here, :], preferred_element_type=jnp.float32
        ).astype(jnp.bfloat16)
        if ahead:
            swap.start(ahead)
    load_pairs.start()
    swap.keep()
    query_sums[...] = jnp.zeros_like(query_sums)
    for at in range(2, EARLY_STEPS):
        line_step(jnp.int32(at))
    swap.wait_recv()
    ones = jnp.ones((8, HEAD_SIZE), jnp.float32)
    for head in range(heads):
        columns = pl.ds(head * HEAD_SIZE, HEAD_SIZE)
        product = mixture[:, columns] * heads_in[:, :, columns].reshape(rows, HEAD_SIZE).astype(
            jnp.float32
        )
        delta[head : head + 1, :] = lax.dot_general(
            ones,
            product,
            (((1,), (1,)), ((), ())),
            precision=lax.Precision.HIGHEST,
            preferred_element_type=jnp.float32,
        )[0:1, :]
    load_pairs.wait()
    lax.fori_loop(0, 2 * chips, turn, 0)

    later = range(EARLY_STEPS + 2 * chips, job.count)
    for at in later[:-1]:
        line_step(jnp.int32(at))
    load_attn_in.start()
    for block in range(count):
        columns = pl.ds(block * width, width)
        for tile in tiles_of(model_width, 768):
            here = pl.ds(block * model_width + tile.start, tile.size)
            wide[here, :] = dot_first(branch_low[:, tile], tokens[:, columns]).astype(jnp.bfloat16)
        save_out[block].start()
    for at in later[-1:]:
        line_step(jnp.int32(at))

    total = part[0, 0].astype(jnp.float32)
    for stage in reversed(range(stages)):
        sum_to_far(1 << stage, stage).wait_recv()
        total = total + from_far[1 << stage].astype(jnp.float32)

    @pl.when(jnp.logical_not(line.is_end))
    def _():
        job.add_middle(job.count - 1)

    def turned_back(grads, first):
        grads = grads.astype(jnp.bfloat16).astype(jnp.float32)
        half_size = HEAD_SIZE // 2
        left_half, right_half = grads[:, :half_size], grads[:, half_size:]
        cos_part = cosine[...].reshape(rows, half_size)
        sin_part = sine[...].reshape(rows, half_size)
        grads_out[:, first : first + half_size] = (
            left_half * cos_part + right_half * sin_part
        ).astype(jnp.bfloat16)
        grads_out[:, first + half_size : first + HEAD_SIZE] = (
            right_half * cos_part - left_half * sin_part
        ).astype(jnp.bfloat16)

    for head in range(heads):
        turned_back(query_sums[:, pl.ds(head * HEAD_SIZE, HEAD_SIZE)], head * HEAD_SIZE)
    turned_back(total[:, :HEAD_SIZE], width)
    grads_out[:, width + HEAD_SIZE :] = total[:, HEAD_SIZE:].astype(jnp.bfloat16)
    load_attn_in.wait()
    for block in range(2):
        save_out[block].wait()
        columns = pl.ds(block * width, width)
        for tile in tiles_of(model_width, 768):
            here = pl.ds(block * model_width + tile.start, tile.size)
            wide[here, :] = dot_first(right[:rows, tile], grads_out[:, columns]).astype(jnp.bfloat16)
        save_columns[block].start()

    @pl.when(line.is_end)
    def _():
        job.close_end()

    @pl.when(jnp.logical_not(line.is_end))
    def _():
        job.finish_middle(job.count - 1)
        job.close_middle()

    for copy in save_columns + save_out[2:] + [move_early]:
        copy.wait()
    swap.wait_send()
    for block in range(chips):
        sum_to_core(block).wait_send()
        if block:
            sum_to_far(block, cube.stage_of(block)).wait_send()


def attention_backward(
    cube, collective_id, grad_model, mid, branch, cotangent, gain_in, gain_out, mixture, query,
    log_total, lower, tokens, cosine, sine, w_out, pairs, left, right, attn_in, early,
):
    count = 4
    tok_rows, model_width = mid.shape
    rows, width = query.shape
    pair_width = pairs.shape[1]
    chips = cube.chips
    heads = width // HEAD_SIZE
    units, ffn_width = left.shape[1], right.shape[1]
    low, full = jnp.bfloat16, jnp.float32
    all_chunks = (units // CHUNK_ROWS, CHUNK_ROWS, ffn_width)
    chunks = (all_chunks[0] - early.shape[0],) + all_chunks[1:]
    inside = pl.BlockSpec(memory_space=pltpu.VMEM)
    outside = pl.BlockSpec(memory_space=pl.ANY)
    wide_rows = max(count * model_width, pairs.shape[0])
    grad_mid, gains, head_grads, out_part, column_part, total = pl.pallas_call(
        functools.partial(attention_backward_kernel, cube),
        out_shape=[
            jax.ShapeDtypeStruct((tok_rows, model_width), full),
            jax.ShapeDtypeStruct((2, model_width), full),
            jax.ShapeDtypeStruct((rows, width + pair_width), low),
            jax.ShapeDtypeStruct((model_width, count * width), low),
            jax.ShapeDtypeStruct((model_width, width + pair_width), low),
            jax.ShapeDtypeStruct(all_chunks, low),
        ],
        in_specs=[inside] * 13 + [outside] * 6,
        out_specs=[inside] * 3 + [outside] * 3,
        scratch_shapes=[
            pltpu.VMEM((tok_rows, model_width), low),
            pltpu.VMEM((wide_rows, width), low),
            pltpu.VMEM(left.shape, low),
            pltpu.VMEM(right.shape, low),
            pltpu.VMEM((chips, 2, rows, pair_width), low),
            pltpu.VMEM((chips, rows, pair_width), low),
            pltpu.VMEM((chips, rows, pair_width), low),
            pltpu.VMEM((rows, width), full),
            pltpu.VMEM((rows, pair_width), full),
            pltpu.VMEM((heads, rows), full),
            pltpu.VMEM((count, tok_rows, width), low),
            pltpu.VMEM((count, tok_rows, width), low),
            pltpu.VMEM(chunks, low),
            pltpu.VMEM(chunks, low),
            pltpu.VMEM(chunks, low),
            pltpu.SemaphoreType.DMA((7, chunks[0])),
            pltpu.SemaphoreType.DMA((5 + count,)),
            pltpu.SemaphoreType.DMA((2 + count,)),
            pltpu.SemaphoreType.DMA((count,)),
            pltpu.SemaphoreType.DMA((count,)),
        ]
        + [pltpu.SemaphoreType.DMA((chips,))] * 4,
        compiler_params=pltpu.CompilerParams(
            collective_id=collective_id,
            has_side_effects=True,
            vmem_limit_bytes=63 * 2**20,
        ),
        cost_estimate=pl.CostEstimate(
            flops=64 * left.shape[0] * units * ffn_width, bytes_accessed=0, transcendentals=0
        ),
    )(
        grad_model,
        mid,
        branch,
        cotangent,
        gain_in.reshape(1, -1),
        gain_out.reshape(1, -1),
        mixture,
        query,
        log_total,
        lower.reshape(1, rows),
        tokens,
        cosine,
        sine,
        w_out,
        pairs,
        left,
        right,
        attn_in,
        early,
    )
    return grad_mid, gains, head_grads, out_part, column_part, total.reshape(units, ffn_width)


class TokenGrads:
    def __init__(self, ins, outs, scratch):
        self.swapped, *self.projections, self.inputs, self.grad_mid, self.gain = ins
        self.grad_inputs, self.gain_sum = outs
        *self.whole, self.landed, self.sums, self.rows, loads, send_sems, recv_sems = scratch
        self.swap = Swap(self.swapped, self.landed, send_sems, recv_sems)
        self.loads = [
            pltpu.make_async_copy(source, target, loads.at[at])
            for at, (source, target) in enumerate(zip(self.projections, self.whole))
        ]
        self.tile = 768
        self.steps = self.sums.shape[1] // self.tile

    def start(self):
        for ahead in range(1, self.swap.count):
            self.swap.start(ahead)
        self.swap.keep()
        for copy in self.loads:
            copy.start()

    def step(self, at):
        @pl.when(at == 0)
        def _():
            self.swap.wait_recv()
            for copy in self.loads:
                copy.wait()
            count = self.swap.count
            first, start = 0, 0
            for weight in self.whole:
                share = weight.shape[1] // count
                for block in range(count):
                    self.rows[:, pl.ds(start + block * share, share)] = self.landed[
                        block, :, pl.ds(first, share)
                    ]
                first, start = first + share, start + count * share

        @pl.when(at >= 0)
        def _():
            features = pl.ds(pl.multiple_of(at * self.tile, self.tile), self.tile)
            start, total = 0, 0.0
            for weight in self.whole:
                total = total + dot_last(
                    self.rows[:, pl.ds(start, weight.shape[1])], weight[features, :]
                )
                start += weight.shape[1]
            self.sums[:, features] = total

    def close(self):
        back, self.gain_sum[...] = norm_backward(
            self.inputs[...].astype(jnp.float32), self.gain[...], self.sums[...]
        )
        self.grad_inputs[...] = self.grad_mid[...] + back
        self.swap.wait_send()


def summed_products_kernel(cube, shares, given_count, spread_count, token_count, *refs):
    refs = list(refs)
    left, right = refs[:2]
    given = refs[2 : 2 + given_count]
    blocks = refs[2 + given_count : 2 + given_count + spread_count]
    refs = refs[2 + given_count + spread_count :]
    token_ins, refs = refs[: 7 * token_count], refs[7 * token_count :]
    if cube:
        small, refs = refs[0], refs[1:]
    outs = refs[: 1 + given_count]
    spread_outs = refs[1 + given_count : 1 + given_count + spread_count]
    refs = refs[1 + given_count + spread_count :]
    token_outs, scratch = refs[: 2 * token_count], refs[2 * token_count :]
    if cube:
        small_out, scratch = scratch[0], scratch[1:]
    line = Line()
    jobs = [
        LineJob(line, *scratch[4 * at : 4 * at + 3], scratch[4 * at + 1], outs[at], scratch[4 * at + 3])
        for at in range(given_count + 1)
    ]
    scratch = scratch[4 * (given_count + 1) :]
    spreads = [
        Spread(
            line, blocks[at], *scratch[3 * at : 3 * at + 2], spread_outs[at], shares,
            scratch[3 * at + 2],
        )
        for at in range(spread_count)
    ]
    scratch = scratch[3 * spread_count :]
    token_scratch, scratch = scratch[: 9 * token_count], scratch[9 * token_count :]
    token = TokenGrads(token_ins, token_outs, token_scratch) if token_count else None
    if cube:
        small_sum, small_in, small_slots, small_send, small_recv, small_spread_sems = scratch
        small_spread = Spread(line, small_sum, small_slots, small_spread_sems)
        cube_devices = [cube.device_across(bit) for bit in [cube.ctx_count] + cube.far_bits]
    for job, before in zip(jobs[1:], jobs):
        job.before = before
    product = jobs[-1]
    per_unit = UNIT_ROWS // product.own.shape[1]

    def each_unit(body):
        def step(unit, carry):
            unit_product(left, right, product.own, unit)
            for part in range(per_unit):
                body(unit * per_unit + part)
            if token:
                token.step(unit - (product.count // per_unit - token.steps))
            return carry

        lax.fori_loop(0, product.count // per_unit, step, 0)

    greet(
        [{"seq": lax.rem(line.place + ahead, 4)} for ahead in range(1, 4)]
        + (cube_devices if cube else [])
    )
    if token:
        token.start()
    for spread in spreads:
        spread.start()
    for array, job in zip(given, jobs):
        job.own[...] = array[...]
    if cube:
        small_sum[...] = small[...]
        for at, device in enumerate(cube_devices):
            copy = remote(
                small_sum, small_in.at[at], small_send.at[at], small_recv.at[at], device
            )
            copy.start()
            copy.wait()
            small_sum[...] += small_in[at]
        small_spread.start()
        spreads = spreads + [small_spread]

    @pl.when(line.is_end)
    def _():
        for job in jobs[:-1]:
            job.each(job.send_end)
        each_unit(product.send_end)
        for spread in spreads:
            spread.forward()
        for job in jobs:
            job.close_end()

    @pl.when(jnp.logical_not(line.is_end))
    def _():
        for spread in spreads:
            spread.forward_turn(1)
        for job in jobs[:-1]:
            job.each(job.add_middle)
        for spread in spreads:
            spread.forward_turn(2)
        each_unit(product.add_middle)
        product.finish_middle(product.count - 1)
        for job in jobs:
            job.close_middle()

    for spread in spreads:
        spread.close()
    if cube:
        small_out[...] = sum(small_slots[at] for at in range(4))
    if token:
        token.close()


def summed_products(
    collective_id, left, right, given=(), blocks=(), shares=(), token=(), small=None, cube=None
):
    rows, units = left.shape
    width = right.shape[1]
    low = jnp.bfloat16
    shapes = [
        (array.shape[0] // GIVEN_ROWS, GIVEN_ROWS, array.shape[1]) for array in given
    ] + [(units // SHORT_CHUNK_ROWS, SHORT_CHUNK_ROWS, width)]
    spreads = [(4,) + block.shape for block in blocks]
    scratch = []
    for shape in shapes:
        scratch += [pltpu.VMEM(shape, low)] * 3 + [pltpu.SemaphoreType.DMA((7, shape[0]))]
    for shape in spreads:
        scratch += [
            pltpu.VMEM(shape, low),
            pltpu.SemaphoreType.DMA((4, 3)),
            pltpu.SemaphoreType.DMA((4 * len(shares),)),
        ]
    spread_outs = [(block.shape[0], 4 * block.shape[1]) for block in blocks]
    out_shapes = [jax.ShapeDtypeStruct(shape, low) for shape in shapes + spread_outs]
    token_specs = []
    inside = pl.BlockSpec(memory_space=pltpu.VMEM)
    outside = pl.BlockSpec(memory_space=pl.ANY)
    outer_count = len(out_shapes)
    if token:
        swapped, projections, inputs = token[0], token[1:4], token[4]
        tok_rows, model_width = inputs.shape
        out_shapes += [
            jax.ShapeDtypeStruct((tok_rows, model_width), jnp.float32),
            jax.ShapeDtypeStruct((1, model_width), jnp.float32),
        ]
        token_specs = [inside] + [outside] * 3 + [inside] * 3
        scratch += [pltpu.VMEM(projection.shape, low) for projection in projections]
        scratch += [
            pltpu.VMEM(swapped.shape, low),
            pltpu.VMEM((tok_rows, model_width), jnp.float32),
            pltpu.VMEM((tok_rows, swapped.shape[0] * swapped.shape[2]), low),
            pltpu.SemaphoreType.DMA((3,)),
            pltpu.SemaphoreType.DMA((4,)),
            pltpu.SemaphoreType.DMA((4,)),
        ]
    extra = []
    if cube:
        extra = [small]
        out_shapes.append(jax.ShapeDtypeStruct(small.shape, small.dtype))
        partners = 1 + cube.stages
        scratch += [
            pltpu.VMEM(small.shape, small.dtype),
            pltpu.VMEM((partners,) + small.shape, small.dtype),
            pltpu.VMEM((4,) + small.shape, small.dtype),
            pltpu.SemaphoreType.DMA((partners,)),
            pltpu.SemaphoreType.DMA((partners,)),
            pltpu.SemaphoreType.DMA((4, 3)),
        ]
    totals = pl.pallas_call(
        functools.partial(
            summed_products_kernel, cube, shares, len(given), len(blocks), 1 if token else 0
        ),
        out_shape=out_shapes,
        in_specs=[inside] * (2 + len(given) + len(blocks))
        + token_specs
        + [inside] * len(extra),
        out_specs=[outside] * outer_count + [inside] * (len(out_shapes) - outer_count),
        scratch_shapes=scratch,
        compiler_params=pltpu.CompilerParams(
            collective_id=collective_id,
            has_side_effects=True,
            vmem_limit_bytes=60 * 2**20,
        ),
        cost_estimate=pl.CostEstimate(
            flops=64 * rows * units * width, bytes_accessed=0, transcendentals=0
        ),
    )(left, right, *(array.reshape(shape) for array, shape in zip(given, shapes)), *blocks, *token, *extra)
    count = len(shapes)
    return [total.reshape(-1, total.shape[-1]) for total in totals[:count]] + list(totals[count:])


def per_device(
    inputs,
    positions,
    w_query,
    key_weight,
    value_weight,
    w_out,
    w_gate,
    w_up,
    w_down,
    gain_attn_in,
    gain_attn_out,
    gain_ffn_in,
    gain_ffn_out,
    cotangent,
):
    layer = ("dp", "ctx")
    tok_rows, model_width = inputs.shape
    seq_count = lax.axis_size("seq")
    seq_index = lax.axis_index("seq")
    cycle_count = lax.axis_size(layer)
    cycle_index = lax.axis_index(layer)
    block_rows = tok_rows * seq_count
    q_width = w_query.shape[1]
    kv_width = key_weight.shape[1]
    q_cols = q_width // seq_count
    kv_cols = kv_width // seq_count
    local_q = q_cols // HEAD_SIZE
    local_kv = kv_cols // HEAD_SIZE
    grouping_factor = local_q // local_kv
    back_blocks = min((WINDOW - 2 + block_rows) // block_rows, cycle_count - 1)
    score_scale = HEAD_SIZE ** (-0.5)

    full_out = gathered(w_out, layer)
    full_key = gathered(key_weight, layer)
    cos_part, sin_part = angles(positions, HEAD_SIZE)
    residual = inputs.astype(jnp.float32)
    row_ids = cycle_index * block_rows + jnp.arange(block_rows, dtype=jnp.int32)
    lower_ids = row_ids - jnp.minimum(positions, WINDOW - 1)
    dp_count, ctx_count = lax.axis_size("dp"), lax.axis_size("ctx")
    fused = (
        seq_count == 4
        and local_kv == 1
        and cube_fits(dp_count, ctx_count, tok_rows, w_gate.shape[0], model_width)
    )
    if fused:
        cube = Cube(dp_count, ctx_count)
        turns = [part.reshape(seq_count, tok_rows, -1) for part in (cos_part, sin_part)]
        block_attn_in, head_weights, query_heads, all_pairs, attn_f32, log_total, out_tok = front(
            cube, 6, inputs, (w_query, key_weight, value_weight), gain_attn_in, *turns, lower_ids
        )
    else:
        own_columns = jnp.concatenate(
            [
                lax.dynamic_slice_in_dim(w_query, seq_index * q_cols, q_cols, 1),
                lax.dynamic_slice_in_dim(key_weight, seq_index * kv_cols, kv_cols, 1),
                lax.dynamic_slice_in_dim(value_weight, seq_index * kv_cols, kv_cols, 1),
            ],
            axis=1,
        )
        block_inputs = gathered(inputs, "seq")
        head_weights = gathered(own_columns, layer)

        block_attn_in = normed(block_inputs.astype(jnp.float32), gain_attn_in).astype(jnp.bfloat16)
        projected = jnp.dot(block_attn_in, head_weights, preferred_element_type=jnp.float32)
        query_heads = rotate(
            projected[:, :q_cols].reshape(block_rows, local_q, HEAD_SIZE), cos_part, sin_part
        ).astype(jnp.bfloat16)
        key_heads = rotate(
            projected[:, q_cols : q_cols + kv_cols].reshape(block_rows, local_kv, HEAD_SIZE),
            cos_part,
            sin_part,
        ).astype(jnp.bfloat16)
        value_heads = projected[:, q_cols + kv_cols :].astype(jnp.bfloat16)
        own_pair = jnp.concatenate([key_heads.reshape(block_rows, kv_cols), value_heads], axis=1)
        all_pairs = gathered(own_pair, layer)
        query_grouped = query_heads.reshape(block_rows, local_kv, grouping_factor, HEAD_SIZE)

        def pair_at(offset):
            if offset == 0:
                pair = own_pair
            else:
                pair = lax.dynamic_slice_in_dim(
                    all_pairs, jnp.maximum(cycle_index - offset, 0) * block_rows, block_rows, 0
                )
            return (
                pair[:, :kv_cols].reshape(block_rows, local_kv, HEAD_SIZE),
                pair[:, kv_cols:].reshape(block_rows, local_kv, HEAD_SIZE),
            )

        kv_pairs = [pair_at(offset) for offset in range(back_blocks + 1)]

        def block_scores(key_rows, offset):
            raw_scores = jnp.einsum(
                "rkgd,ckd->kgrc", query_grouped, key_rows, preferred_element_type=jnp.float32
            )
            capped = SOFT_CAP * jnp.tanh(raw_scores * score_scale / SOFT_CAP)
            col_ids = (cycle_index - offset) * block_rows + jnp.arange(block_rows, dtype=jnp.int32)
            allowed = (col_ids[None, :] <= row_ids[:, None]) & (col_ids[None, :] >= lower_ids[:, None])
            return (capped, allowed)

        capped, allowed = block_scores(kv_pairs[0][0], 0)
        row_top = jnp.max(jnp.where(allowed, capped, -1e30), axis=-1)
        running_sum = jnp.sum(jnp.where(allowed, jnp.exp(capped - row_top[..., None]), 0.0), axis=-1)
        for offset in range(1, back_blocks + 1):
            capped, allowed = block_scores(kv_pairs[offset][0], offset)
            new_top = jnp.maximum(row_top, jnp.max(jnp.where(allowed, capped, -1e30), axis=-1))
            running_sum = running_sum * jnp.exp(row_top - new_top) + jnp.sum(
                jnp.where(allowed, jnp.exp(capped - new_top[..., None]), 0.0), axis=-1
            )
            row_top = new_top
        log_total = row_top + jnp.log(running_sum)
        mixture = jnp.zeros((block_rows, local_kv, grouping_factor, HEAD_SIZE), jnp.float32)
        for offset in range(back_blocks + 1):
            capped, allowed = block_scores(kv_pairs[offset][0], offset)
            probs_low = jnp.where(allowed, jnp.exp(capped - log_total[..., None]), 0.0).astype(
                jnp.bfloat16
            )
            mixture = mixture + jnp.einsum(
                "kgrc,ckd->rkgd", probs_low, kv_pairs[offset][1], preferred_element_type=jnp.float32
            )
        attn_f32 = mixture.reshape(block_rows, q_cols)
        out_tok = lax.all_to_all(
            attn_f32.astype(jnp.bfloat16), "seq", split_axis=0, concat_axis=1, tiled=True
        )
    branch = dot_last(out_tok, full_out)
    mid = residual + normed(branch, gain_attn_out)

    weights = (w_gate, w_up, w_down)
    ffn_own = normed(mid, gain_ffn_in).astype(jnp.bfloat16)
    (ffn_own,) = after((ffn_own,), (full_key,))
    if fused:
        ffn_out, ffn_in, hidden, activated, slope = ffn_call(
            ffn_forward_kernel, cube, 1, ffn_own, weights, (), 3
        )
    else:
        ffn_in = gathered(ffn_own, layer)
        gate_pre = dot_last(ffn_in, w_gate)
        up_pre = dot_last(ffn_in, w_up)
        activated, gelu_pull = jax.vjp(gelu_tanh, gate_pre)
        slope = gelu_pull(up_pre)[0]
        hidden = (activated * up_pre).astype(jnp.bfloat16)
        ffn_out = scattered(jnp.dot(hidden, w_down, preferred_element_type=jnp.float32), layer)
    grad_out = cotangent.astype(jnp.float32)
    ffn_norm, pull_ffn = jax.vjp(normed, ffn_out, gain_ffn_out)
    output = mid + ffn_norm
    grad_ffn, grad_gain_ffn_out = pull_ffn(grad_out)
    grad_ffn_own = grad_ffn.astype(jnp.bfloat16)
    if fused:
        grad_model, grad_ffn_low, grad_gate, grad_up, early_down = ffn_call(
            ffn_backward_kernel, cube, 2, grad_ffn_own, weights, (activated, slope), 2, (hidden,)
        )
        early_down = early_down.reshape(-1, CHUNK_ROWS, model_width)
    else:
        grad_ffn_low = gathered(grad_ffn_own, layer)
        grad_hidden = dot_last(grad_ffn_low, w_down)
        grad_gate = (grad_hidden * slope).astype(jnp.bfloat16)
        grad_up = (grad_hidden * activated).astype(jnp.bfloat16)
        grad_model = scattered(
            jnp.dot(grad_gate, w_gate, preferred_element_type=jnp.float32)
            + jnp.dot(grad_up, w_up, preferred_element_type=jnp.float32),
            layer,
        )
    ffn_in, grad_ffn_low, hidden, grad_gate, grad_up = (
        rows.reshape(-1, rows.shape[-1])
        for rows in (ffn_in, grad_ffn_low, hidden, grad_gate, grad_up)
    )
    if fused:
        grad_mid, gains, head_grads, grad_w_out_part, column_part, grad_w_down = attention_backward(
            cube, 3, grad_model, mid, branch, cotangent, gain_ffn_in, gain_attn_out, attn_f32,
            query_heads, log_total, lower_ids, out_tok, *turns, full_out, all_pairs, hidden, grad_ffn_low,
            block_attn_in, early_down,
        )
        grad_gain_ffn_in, grad_gain_attn_out = gains[0], gains[1]
    else:
        mid_norm, pull_mid = jax.vjp(normed, mid, gain_ffn_in)
        grad_mid_part, grad_gain_ffn_in = pull_mid(grad_model)
        grad_mid = grad_out + grad_mid_part
        branch_norm, pull_branch = jax.vjp(normed, branch, gain_attn_out)
        grad_branch, grad_gain_attn_out = pull_branch(grad_mid)
        grad_branch_low = grad_branch.astype(jnp.bfloat16)
        grad_attn_tok = jnp.dot(grad_branch_low, full_out, preferred_element_type=jnp.float32).astype(
            jnp.bfloat16
        )
        grad_attn_heads = lax.all_to_all(grad_attn_tok, "seq", split_axis=1, concat_axis=0, tiled=True)
        grad_grouped = grad_attn_heads.reshape(block_rows, local_kv, grouping_factor, HEAD_SIZE)
        out_grouped = attn_f32.reshape(block_rows, local_kv, grouping_factor, HEAD_SIZE)
        row_delta = jnp.transpose(
            jnp.sum(grad_grouped.astype(jnp.float32) * out_grouped, axis=-1), (1, 2, 0)
        )
        grad_query = jnp.zeros((block_rows, local_kv, grouping_factor, HEAD_SIZE), jnp.float32)
        kv_grads = jnp.zeros(((back_blocks + cycle_count) * block_rows, 2 * kv_cols), jnp.bfloat16)
        for offset in range(back_blocks, -1, -1):
            key_rows, value_rows = kv_pairs[offset]
            capped, allowed = block_scores(key_rows, offset)
            probs = jnp.where(allowed, jnp.exp(capped - log_total[..., None]), 0.0)
            grad_value = jnp.einsum(
                "kgrc,rkgd->ckd",
                probs.astype(jnp.bfloat16),
                grad_grouped,
                preferred_element_type=jnp.float32,
            )
            grad_probs = jnp.einsum(
                "rkgd,ckd->kgrc", grad_grouped, value_rows, preferred_element_type=jnp.float32
            )
            cap_ratio = capped / SOFT_CAP
            grad_raw = (
                probs
                * (grad_probs - row_delta[..., None])
                * (1.0 - cap_ratio * cap_ratio)
                * score_scale
            ).astype(jnp.bfloat16)
            grad_query = grad_query + jnp.einsum(
                "kgrc,ckd->rkgd", grad_raw, key_rows, preferred_element_type=jnp.float32
            )
            grad_key = jnp.einsum(
                "kgrc,rkgd->ckd", grad_raw, query_grouped, preferred_element_type=jnp.float32
            )
            grad_term = jnp.concatenate(
                [grad_key.reshape(block_rows, kv_cols), grad_value.reshape(block_rows, kv_cols)], axis=1
            )
            kv_grads = lax.dynamic_update_slice_in_dim(
                kv_grads,
                grad_term.astype(jnp.bfloat16),
                (cycle_index - offset + back_blocks) * block_rows,
                0,
            )
        kv_share = scattered_low(kv_grads[back_blocks * block_rows :], layer)
        grad_query = grad_query.reshape(block_rows, q_cols).astype(jnp.bfloat16)
        grad_w_down = summed(dot_first(hidden, grad_ffn_low), "seq")
        grad_w_out_part = dot_first(grad_branch_low, out_tok).astype(jnp.bfloat16)
        kv_share = kv_share.astype(jnp.float32)
        grad_q_pre = rotate_back(
            grad_query.astype(jnp.float32).reshape(block_rows, local_q, HEAD_SIZE),
            cos_part,
            sin_part,
        ).reshape(block_rows, q_cols)
        grad_k_pre = rotate_back(
            kv_share[:, :kv_cols].reshape(block_rows, local_kv, HEAD_SIZE), cos_part, sin_part
        ).reshape(block_rows, kv_cols)
        head_grads = jnp.concatenate([grad_q_pre, grad_k_pre, kv_share[:, kv_cols:]], axis=1).astype(
            jnp.bfloat16
        )
        column_part = dot_first(block_attn_in, head_grads).astype(jnp.bfloat16)
    if fused:
        full_query, full_value = (
            gathered(weight, layer) for weight in after((w_query, value_weight), (grad_model,))
        )
        full_weights = [full_query, full_key, full_value]
        grad_w_gate, grad_inputs, grad_gain_attn_in = summed_products(
            4,
            *after(
                (grad_gate, ffn_in),
                (grad_w_down, column_part, grad_w_out_part, *full_weights),
            ),
            token=(
                head_grads.reshape(seq_count, tok_rows, -1),
                *full_weights,
                inputs,
                grad_mid,
                gain_attn_in.reshape(1, -1),
            ),
        )
        grad_gain_attn_in = grad_gain_attn_in[0]
    else:
        grad_w_gate = summed(dot_first(grad_gate, ffn_in), "seq")
        grad_attn_in = scattered(dot_last(head_grads, head_weights), "seq")
        in_norm, pull_in = jax.vjp(normed, residual, gain_attn_in)
        grad_res_part, grad_gain_attn_in = pull_in(grad_attn_in)
        grad_inputs = grad_mid + grad_res_part
    grad_w_out, column_share = after(
        (scattered_low(grad_w_out_part, layer), scattered_low(column_part, layer)), (grad_w_gate,)
    )
    gain_rows = jnp.stack(
        [grad_gain_attn_in, grad_gain_attn_out, grad_gain_ffn_in, grad_gain_ffn_out]
    )
    if fused:
        grad_w_out, grad_w_up, column_grads, gain_grads = summed_products(
            5,
            *after((grad_up, ffn_in), (grad_w_gate, grad_inputs)),
            (grad_w_out,),
            (column_share,),
            (q_cols, kv_cols, kv_cols),
            small=gain_rows,
            cube=cube,
        )
    else:
        grad_w_up = summed(dot_first(grad_up, ffn_in), "seq")
        grad_w_out = summed(grad_w_out, "seq")
        column_grads = jnp.concatenate(
            [
                lax.all_gather(column_share[:, first : first + share], "seq", axis=1, tiled=True)
                for first, share in ((0, q_cols), (q_cols, kv_cols), (q_cols + kv_cols, kv_cols))
            ],
            axis=1,
        )
        gain_grads = lax.psum(gain_rows, ("dp", "ctx", "seq"))
    column_grads = column_grads.astype(jnp.float32)
    grad_w_gate, grad_w_down = after((grad_w_gate, grad_w_down), (grad_w_up,))
    grad_w_out, grad_w_gate, grad_w_up, grad_w_down = (
        grad.astype(jnp.float32) for grad in (grad_w_out, grad_w_gate, grad_w_up, grad_w_down)
    )
    return (
        output,
        grad_inputs,
        column_grads[:, :q_width],
        column_grads[:, q_width : q_width + kv_width],
        column_grads[:, q_width + kv_width :],
        grad_w_out,
        grad_w_gate,
        grad_w_up,
        grad_w_down,
        gain_grads[0],
        gain_grads[1],
        gain_grads[2],
        gain_grads[3],
    )


def solution(mesh):
    placed = (
        P(("dp", "ctx", "seq"), None),
        P(("dp", "ctx")),
        P(("dp", "ctx"), None),
        P(("dp", "ctx"), None),
        P(("dp", "ctx"), None),
        P(("dp", "ctx"), None),
        P(("dp", "ctx"), None),
        P(("dp", "ctx"), None),
        P(("dp", "ctx"), None),
        P(),
        P(),
        P(),
        P(),
        P(("dp", "ctx", "seq"), None),
    )
    return jax.shard_map(
        per_device,
        mesh=mesh,
        in_specs=placed,
        out_specs=(
            P(("dp", "ctx", "seq"), None),
            P(("dp", "ctx", "seq"), None),
            P(("dp", "ctx"), None),
            P(("dp", "ctx"), None),
            P(("dp", "ctx"), None),
            P(("dp", "ctx"), None),
            P(("dp", "ctx"), None),
            P(("dp", "ctx"), None),
            P(("dp", "ctx"), None),
            P(),
            P(),
            P(),
            P(),
        ),
        check_vma=False,
    )
```
